32 devices in a mesh: gx: 4 (over y, x), gy: 8 (over z, core).
Axes of the slice: x: 2, y: 2, z: 4, core: 2. Of those that a mesh axis runs over, the one named last changes fastest.
Arguments:
- samples: float32 [2048, 512], replicated, may hold values from -1 to 1
- real_idx: int32 [8, 8, 256], P('gx', 'gy'), may hold values from 0 to 2047
- latents: float32 [8, 8, 256, 512], P('gx', 'gy'), may hold values from -6 to 6
- gen_weight: float32 [8, 8, 512, 512], P('gx', 'gy'), may hold values from -6 to 6
- disc_weight: float32 [8, 8, 512, 512], P('gx', 'gy'), may hold values from -6 to 6
- disc_head: float32 [8, 8, 512], P('gx', 'gy'), may hold values from -6 to 6
Outputs:
- new_gen: float32 [8, 8, 512, 512], P('gx', 'gy')
- new_disc: float32 [8, 8, 512, 512], P('gx', 'gy')
- new_head: float32 [8, 8, 512], P('gx', 'gy')
The draws below stay inside these ranges and needn't reach their ends.
All inputs are finite; a program needn't handle non-finite values.
Results may differ from the reference program's by a relative error of at most 0.0001.
Values sent between devices are 32-bit elements; how exact they have to be, the bound alone decides.
A program may use at most 128 MiB of HBM per device.

```python
import jax
import jax.numpy as jnp
from jax import lax

W = 512
ROWS = 256
TABLE = 2048
NX = 8
NY = 8


def place_ends(entries, own_key, low, top_value):
    longest = entries.shape.index(max(entries.shape))
    spots = []
    for shift in (0, 1):
        where = [jax.random.randint(jax.random.fold_in(own_key, axis), (), 0, length) for axis, length in enumerate(entries.shape)]
        where[longest] = (where[longest] + shift) % entries.shape[longest]
        spots.append(tuple(where))
    return entries.at[spots[0]].set(low).at[spots[1]].set(top_value)


def block_scale(stream_key, shape, pieces, smallest, high):
    level = 1.0
    for dim, parts in pieces:
        heights = jax.random.uniform(jax.random.fold_in(jax.random.fold_in(stream_key, 6), dim), (parts,), jnp.float32, smallest / len(pieces), high / len(pieces))
        level = level * jnp.repeat(jnp.exp(heights), shape[dim] // parts).reshape((-1,) + (1,) * (len(shape) - 1 - dim))
    return level


def bell_draw(stream_key, extent, width, most, pieces=(), held_as=jnp.bfloat16):
    drawn = jax.random.normal(stream_key, extent, jnp.float32) * width
    if len(pieces) > 0:
        drawn = block_scale(stream_key, extent, pieces, -0.22, 0.18) * drawn
    return jnp.clip(drawn, min=-most, max=most).astype(held_as)


def setup_inputs(seed: int = 0) -> dict:
    seeds = jax.random.split(jax.random.key(seed), 7)
    return {
        "samples": jnp.clip(jax.random.uniform(seeds[0], (TABLE, W), jnp.float32, -1.0, 1.0), -1.0, 1.0),
        "real_idx": place_ends(jax.random.randint(seeds[1], (NX, NY, ROWS), 0, TABLE), jax.random.fold_in(seeds[1], 1), 0, TABLE - 1).astype(jnp.int32),
        "latents": bell_draw(seeds[2], (NX, NY, ROWS, W), 1.0, 6.0, ((0, 4), (1, 8)), jnp.float32),
        "gen_weight": bell_draw(seeds[3], (NX, NY, W, W), 1.0, 6.0, ((0, 4), (1, 8)), jnp.float32),
        "disc_weight": bell_draw(seeds[4], (NX, NY, W, W), 1.0, 6.0, ((0, 4), (1, 8)), jnp.float32),
        "disc_head": bell_draw(seeds[5], (NX, NY, W), 1.0, 6.0, ((0, 4), (1, 8)), jnp.float32),
    }


HIGH = lax.Precision.HIGHEST

def product(left, right):
    return jnp.einsum('xybk,xykn->xybn', left, right, precision=HIGH)

def beside_all(field):
    return [field, jnp.roll(field, 1, 0), jnp.roll(field, -1, 0), jnp.roll(field, 1, 1), jnp.roll(field, -1, 1)]

def opponent(fake, weight, head, scale):
    hidden = jnp.tanh(scale * product(fake, weight))
    score = scale * jnp.einsum('xybn,xyn->xyb', hidden, head, precision=HIGH)
    slope = -jax.nn.sigmoid(-score)
    inner = (1.0 - hidden * hidden) * (scale * slope[..., None] * head[:, :, None, :])
    return scale * jnp.einsum('xybn,xykn->xybk', inner, weight, precision=HIGH)

def critic(inputs, weight, head, scale, real_side):
    hidden = jnp.tanh(scale * product(inputs, weight))
    score = scale * jnp.einsum('xybn,xyn->xyb', hidden, head, precision=HIGH)
    if real_side:
        slope = -jax.nn.sigmoid(-score)
    else:
        slope = 0.2 * jax.nn.sigmoid(score)
    inner = (1.0 - hidden * hidden) * (scale * slope[..., None] * head[:, :, None, :])
    grad_w = scale * jnp.einsum('xybk,xybn->xykn', inputs, inner, precision=HIGH)
    grad_h = scale * jnp.einsum('xyb,xybn->xyn', slope, hidden, precision=HIGH)
    return (grad_w, grad_h)

def descend(value, grad, axes):
    mean_sq = lax.optimization_barrier(jnp.mean(grad * grad, axis=axes, keepdims=True))
    return value - 0.25 * grad * lax.rsqrt(mean_sq + 1e-06)

def reference(samples, real_idx, latents, gen_weight, disc_weight, disc_head):
    scale = W ** (-0.5)
    fake = jnp.tanh(scale * product(latents, gen_weight))
    back = jnp.zeros_like(fake)
    for weight, head in zip(beside_all(disc_weight), beside_all(disc_head)):
        back = back + opponent(fake, weight, head, scale)
    gen_grad = scale * jnp.einsum('xybk,xybn->xykn', latents, (1.0 - fake * fake) * back, precision=HIGH)
    new_gen = descend(gen_weight, gen_grad, (2, 3))
    real = jnp.take(samples, real_idx, axis=0)
    grad_w, grad_h = critic(real, disc_weight, disc_head, scale, True)
    for generator in beside_all(new_gen):
        made = jnp.tanh(scale * product(latents, generator))
        term_w, term_h = critic(made, disc_weight, disc_head, scale, False)
        grad_w = grad_w + term_w
        grad_h = grad_h + term_h
    new_disc = descend(disc_weight, grad_w, (2, 3))
    new_head = descend(disc_head, grad_h, (2,))
    return (new_gen, new_disc, new_head)
```

```python
import jax
import jax.numpy as jnp
from jax import lax
from jax.sharding import PartitionSpec as P

HIGH = lax.Precision.HIGH


def dot(left, right, dims):
    return lax.dot_general(left, right, (dims, ((), ())), precision=HIGH)


def moved(value, axis, by):
    count = lax.axis_size(axis)
    return lax.ppermute(value, axis, [(i, (i + by) % count) for i in range(count)])


def sides_of(cells):
    nx, ny = len(cells), len(cells[0])
    right = [moved(row[ny - 1], "gy", 1) for row in cells]
    left = [moved(row[0], "gy", -1) for row in cells]
    top = [moved(c, "gx", 1) for c in cells[nx - 1]]
    bottom = [moved(c, "gx", -1) for c in cells[0]]
    grid = lambda f: [[f(i, j) for j in range(ny)] for i in range(nx)]
    return [
        grid(lambda i, j: cells[i - 1][j] if i > 0 else top[j]),
        grid(lambda i, j: cells[i + 1][j] if i + 1 < nx else bottom[j]),
        grid(lambda i, j: cells[i][j - 1] if j > 0 else right[i]),
        grid(lambda i, j: cells[i][j + 1] if j + 1 < ny else left[i]),
    ]


def returned(grids):
    up, down, before, after = grids
    nx, ny = len(up), len(up[0])
    from_after = [moved(before[i][0], "gy", -1) for i in range(nx)]
    from_before = [moved(after[i][ny - 1], "gy", 1) for i in range(nx)]
    from_below = [moved(up[0][j], "gx", -1) for j in range(ny)]
    from_above = [moved(down[nx - 1][j], "gx", 1) for j in range(ny)]
    grid = lambda f: [[f(i, j) for j in range(ny)] for i in range(nx)]
    return [
        grid(lambda i, j: up[i + 1][j] if i + 1 < nx else from_below[j]),
        grid(lambda i, j: down[i - 1][j] if i > 0 else from_above[j]),
        grid(lambda i, j: before[i][j + 1] if j + 1 < ny else from_after[i]),
        grid(lambda i, j: after[i][j - 1] if j > 0 else from_before[i]),
    ]


def opponent(fake, weight, head, scale):
    hidden = jnp.tanh(scale * dot(fake, weight, ((1,), (0,))))
    score = scale * jnp.sum(hidden * head, -1, keepdims=True)
    inner = (1.0 - hidden * hidden) * ((scale * -jax.nn.sigmoid(-score)) * head)
    return scale * dot(inner, weight, ((1,), (1,)))


def critic(inputs, weight, head, scale, real_side):
    hidden = jnp.tanh(scale * dot(inputs, weight, ((1,), (0,))))
    score = scale * jnp.sum(hidden * head, -1, keepdims=True)
    slope = -jax.nn.sigmoid(-score) if real_side else 0.2 * jax.nn.sigmoid(score)
    inner = (1.0 - hidden * hidden) * ((scale * slope) * head)
    return scale * dot(inputs, inner, ((0,), (0,))), scale * jnp.sum(slope * hidden, 0, keepdims=True)


def descend(value, grad):
    return value - 0.25 * grad * lax.rsqrt(jnp.mean(grad * grad) + 1e-06)


def local(samples, real_idx, latents, gen_weight, disc_weight, disc_head):
    nx, ny, rows, width = latents.shape
    scale = width ** (-0.5)
    cut = lambda a: [[a[i, j] for j in range(ny)] for i in range(nx)]
    lat, gen, disc = cut(latents), cut(gen_weight), cut(disc_weight)
    head = [[disc_head[i, j][None] for j in range(ny)] for i in range(nx)]
    disc_sides, head_sides = sides_of(disc), sides_of(head)
    lat_sides = sides_of(lat)
    spots = [(i, j) for i in range(nx) for j in range(ny)]
    new_gen = [[None] * ny for _ in range(nx)]
    grads = [[None] * ny for _ in range(nx)]
    for i, j in spots:
        real = jnp.take(samples, real_idx[i, j], axis=0)
        grads[i][j] = critic(real, disc[i][j], head[i][j], scale, True)
    fakes = [[jnp.tanh(scale * dot(lat[i][j], gen[i][j], ((1,), (0,)))) for j in range(ny)] for i in range(nx)]
    for i, j in spots:
        fake = fakes[i][j]
        back = opponent(fake, disc[i][j], head[i][j], scale)
        for d, h in zip(disc_sides, head_sides):
            back = back + opponent(fake, d[i][j], h[i][j], scale)
        grad = scale * dot(lat[i][j], (1.0 - fake * fake) * back, ((0,), (0,)))
        new_gen[i][j] = descend(gen[i][j], grad)
    make = lambda side: [
        [jnp.tanh(scale * dot(side[i][j], new_gen[i][j], ((1,), (0,)))) for j in range(ny)] for i in range(nx)
    ]
    made = [make(lat)] + returned([make(side) for side in lat_sides])
    new_disc = [[None] * ny for _ in range(nx)]
    new_head = [[None] * ny for _ in range(nx)]
    for i, j in spots:
        grad_w, grad_h = grads[i][j]
        for m in made:
            term_w, term_h = critic(m[i][j], disc[i][j], head[i][j], scale, False)
            grad_w, grad_h = grad_w + term_w, grad_h + term_h
        new_disc[i][j] = descend(disc[i][j], grad_w)
        new_head[i][j] = descend(head[i][j], grad_h)[0]
    join = lambda grid: jnp.stack([jnp.stack(row) for row in grid])
    return join(new_gen), join(new_disc), join(new_head)


def solution(mesh):
    cells3, cells4 = P("gx", "gy", None), P("gx", "gy", None, None)
    return jax.shard_map(
        local,
        mesh=mesh,
        in_specs=(P(), cells3, cells4, cells4, cells4, cells3),
        out_specs=(cells4, cells4, cells3),
        check_vma=False,
    )
```

```python
import functools

import jax
import jax.numpy as jnp
from jax import lax
from jax.experimental import pallas as pl
from jax.experimental.pallas import tpu as pltpu
from jax.sharding import PartitionSpec as P

F32 = jnp.float32
NN = ((1,), (0,))
NT = ((1,), (1,))
TN = ((0,), (0,))


def split(x):
    high = x.astype(jnp.bfloat16)
    return high, (x - high.astype(F32)).astype(jnp.bfloat16)


def dot3(a, b, dims):
    d = lambda x, y: lax.dot_general(x, y, (dims, ((), ())), preferred_element_type=F32)
    return d(a[0], b[0]) + (d(a[0], b[1]) + d(a[1], b[0]))


def descend(value, grad):
    mean_sq = jnp.sum(jnp.sum(grad * grad, 0, keepdims=True), 1, keepdims=True) * (1.0 / grad.size)
    return value - 0.25 * grad * lax.rsqrt(mean_sq + 1e-06)


def kernel(
    nx, ny, gxn, gyn,
    samples, idx, lat, gen, disc, head,
    new_gen, new_disc, new_head,
    table, real, disc_h, head_h, lat_h, made_in, made_out, fake, back, gw, gh, whi, wlo,
    table_sem, disc_s, disc_r, head_s, head_r, lat_s, lat_r, made_s, made_r,
):
    cells, rows, width = lat.shape
    slots = 2 * nx + 2 * ny
    scale = width ** (-0.5)
    gx, gy = lax.axis_index("gx"), lax.axis_index("gy")
    above, below = lax.rem(gx + gxn - 1, gxn), lax.rem(gx + 1, gxn)
    before, after = lax.rem(gy + gyn - 1, gyn), lax.rem(gy + 1, gyn)

    table_copy = pltpu.make_async_copy(samples, table, table_sem)
    table_copy.start()

    barrier = pltpu.get_barrier_semaphore()
    for there in ({"gx": above}, {"gx": below}, {"gy": before}, {"gy": after}):
        pl.semaphore_signal(barrier, inc=1, device_id=there, device_id_type=pl.DeviceIdType.MESH)
    pl.semaphore_wait(barrier, 4)

    def remote(src, dst, send, recv, there):
        return pltpu.make_async_remote_copy(
            src_ref=src, dst_ref=dst, send_sem=send, recv_sem=recv,
            device_id=there, device_id_type=pl.DeviceIdType.MESH,
        )

    outgoing = []
    for i in range(nx):
        outgoing.append((2 * ny + i, i * ny + ny - 1, {"gy": after}))
        outgoing.append((2 * ny + nx + i, i * ny, {"gy": before}))
    for j in range(ny):
        outgoing.append((j, (nx - 1) * ny + j, {"gx": below}))
        outgoing.append((ny + j, j, {"gx": above}))

    head_out = [remote(head.at[c], head_h.at[s], head_s.at[s], head_r.at[s], t) for s, c, t in outgoing]
    disc_out = [remote(disc.at[c], disc_h.at[s], disc_s.at[s], disc_r.at[s], t) for s, c, t in outgoing]
    lat_out = [remote(lat.at[c], lat_h.at[s], lat_s.at[s], lat_r.at[s], t) for s, c, t in outgoing]
    for h, d in zip(head_out, disc_out):
        h.start()
        d.start()

    def arrived(buf, sem, s):
        remote(buf.at[s], buf.at[s], sem.at[s], sem.at[s], {"gx": above}).wait_recv()

    def row_slot(t):
        d, i = lax.rem(t // nx + gy + 1, 2), lax.rem(t, nx)
        return d, 2 * ny + d * nx + i, 2 * ny + (1 - d) * nx + i, i * ny + d * (ny - 1)

    def col_slot(t):
        d, j = t // ny, lax.rem(t, ny)
        return d, d * ny + j, (1 - d) * ny + j, d * (nx - 1) * ny + j

    pair_loops = []
    if nx > 1:
        half = (nx - 1) * ny
        def vertical(t, half=half):
            b, d = lax.rem(t, half), t // half
            return b + d * ny, b + (1 - d) * ny
        pair_loops.append((2 * half, vertical))
    if ny > 1:
        wide = nx * (ny - 1)
        def horizontal(t, wide=wide):
            b, d = lax.rem(t, wide), t // wide
            at = (b // (ny - 1)) * ny + lax.rem(b, ny - 1)
            return at + d, at + 1 - d
        pair_loops.append((2 * wide, horizontal))

    def slope_inner(hidden, top, real_side):
        score = scale * jnp.sum(hidden * top, 1, keepdims=True)
        slope = -jax.nn.sigmoid(-score) if real_side else 0.2 * jax.nn.sigmoid(score)
        return slope, (1.0 - hidden * hidden) * ((scale * slope) * top)

    def opponent(x, w, top):
        hidden = jnp.tanh(scale * dot3(split(x), w, NN))
        _, inner = slope_inner(hidden, top, True)
        return scale * dot3(split(inner), w, NT)

    def critic(x, c, real_side):
        xs = split(x)
        top = head[c]
        hidden = jnp.tanh(scale * dot3(xs, (whi[c], wlo[c]), NN))
        slope, inner = slope_inner(hidden, top, real_side)
        return scale * dot3(xs, split(inner), TN), scale * jnp.sum(slope * hidden, 0, keepdims=True)

    def add_critic(x, c):
        term_w, term_h = critic(x, c, False)
        gw[c] += term_w
        gh[c] += term_h

    def make(source, g):
        return jnp.tanh(scale * dot3(split(source), split(new_gen[g]), NN))

    def own(c, _):
        whi[c], wlo[c] = split(disc[c])
        fake[c] = jnp.tanh(scale * dot3(split(lat[c]), split(gen[c]), NN))
        back[c] = opponent(fake[c], (whi[c], wlo[c]), head[c])
        return 0

    lax.fori_loop(0, cells, own, 0)
    for count, pair in pair_loops:
        def local_opponent(t, _, pair=pair):
            c, n = pair(t)
            back[c] += opponent(fake[c], (whi[n], wlo[n]), head[n])
            return 0
        lax.fori_loop(0, count, local_opponent, 0)

    table_copy.wait()

    def real_term(c, _):
        def fetch(b, _):
            for k in range(8):
                r = b * 8 + k
                real[pl.ds(r, 1), :] = table[pl.ds(idx[c, r], 1), :]
            return 0
        lax.fori_loop(0, rows // 8, fetch, 0)
        gw[c], gh[c] = critic(real[...], c, True)
        return 0

    lax.fori_loop(0, cells, real_term, 0)

    def far_opponent(where):
        def body(t, _):
            _, s, _, c = where(t)
            arrived(head_h, head_r, s)
            arrived(disc_h, disc_r, s)
            back[c] += opponent(fake[c], split(disc_h[s]), head_h[s])
            return 0
        return body

    for h, d, l in zip(head_out, disc_out, lat_out):
        h.wait_send()
        d.wait_send()
        l.start()
    lax.fori_loop(0, 2 * nx, far_opponent(row_slot), 0)
    lax.fori_loop(0, 2 * ny, far_opponent(col_slot), 0)

    def update(c, _):
        f = fake[c]
        grad = scale * dot3(split(lat[c]), split((1.0 - f * f) * back[c]), TN)
        new_gen[c] = descend(gen[c], grad)
        return 0

    lax.fori_loop(0, cells, update, 0)

    def made_copy(where, axis, t):
        d, s, there, _ = where(t)
        me, n = (gx, gxn) if axis == "gx" else (gy, gyn)
        target = lax.rem(me + n + 2 * d - 1, n)
        return remote(made_out.at[s], made_in.at[there], made_s.at[s], made_r.at[there], {axis: target})

    def far_make(where, axis):
        def body(t, _):
            _, s, _, c = where(t)
            arrived(lat_h, lat_r, s)
            made_out[s] = make(lat_h[s], c)
            made_copy(where, axis, t).start()
            return 0
        return body

    lax.fori_loop(0, 2 * nx, far_make(row_slot, "gy"), 0)
    lax.fori_loop(0, 2 * ny, far_make(col_slot, "gx"), 0)

    def own_critic(c, _):
        add_critic(make(lat[c], c), c)
        return 0

    lax.fori_loop(0, cells, own_critic, 0)
    for count, pair in pair_loops:
        def local_critic(t, _, pair=pair):
            c, n = pair(t)
            add_critic(make(lat[c], n), c)
            return 0
        lax.fori_loop(0, count, local_critic, 0)

    def far_critic(where):
        def body(t, _):
            _, s, _, c = where(t)
            arrived(made_in, made_r, s)
            add_critic(made_in[s], c)
            return 0
        return body

    lax.fori_loop(0, 2 * nx, far_critic(row_slot), 0)
    lax.fori_loop(0, 2 * ny, far_critic(col_slot), 0)

    def finish(c, _):
        new_disc[c] = descend(disc[c], gw[c])
        new_head[c] = descend(head[c], gh[c])
        return 0

    lax.fori_loop(0, cells, finish, 0)
    for l in lat_out:
        l.wait_send()
    for t in range(2 * nx):
        made_copy(row_slot, "gy", t).wait_send()
    for t in range(2 * ny):
        made_copy(col_slot, "gx", t).wait_send()


def local(gxn, gyn, samples, real_idx, latents, gen_weight, disc_weight, disc_head):
    nx, ny, rows, width = latents.shape
    cells, slots = nx * ny, 2 * (nx + ny)
    vmem = pl.BlockSpec(memory_space=pltpu.VMEM)
    square, block, line = (width, width), (rows, width), (1, width)
    dma = lambda: pltpu.SemaphoreType.DMA((slots,))
    outs = pl.pallas_call(
        functools.partial(kernel, nx, ny, gxn, gyn),
        out_shape=(
            jax.ShapeDtypeStruct((cells,) + square, F32),
            jax.ShapeDtypeStruct((cells,) + square, F32),
            jax.ShapeDtypeStruct((cells,) + line, F32),
        ),
        in_specs=[pl.BlockSpec(memory_space=pl.ANY), pl.BlockSpec(memory_space=pltpu.SMEM)] + [vmem] * 4,
        out_specs=(vmem, vmem, vmem),
        scratch_shapes=[
            pltpu.VMEM(samples.shape, F32),
            pltpu.VMEM(block, F32),
            pltpu.VMEM((slots,) + square, F32),
            pltpu.VMEM((slots,) + line, F32),
            pltpu.VMEM((slots,) + block, F32),
            pltpu.VMEM((slots,) + block, F32),
            pltpu.VMEM((slots,) + block, F32),
            pltpu.VMEM((cells,) + block, F32),
            pltpu.VMEM((cells,) + block, F32),
            pltpu.VMEM((cells,) + square, F32),
            pltpu.VMEM((cells,) + line, F32),
            pltpu.VMEM((cells,) + square, jnp.bfloat16),
            pltpu.VMEM((cells,) + square, jnp.bfloat16),
            pltpu.SemaphoreType.DMA,
        ] + [dma() for _ in range(8)],
        compiler_params=pltpu.CompilerParams(
            collective_id=0, has_side_effects=True, vmem_limit_bytes=58 * 1024 * 1024
        ),
        name="coev",
    )(
        samples,
        real_idx.reshape(cells, rows),
        latents.reshape((cells,) + block),
        gen_weight.reshape((cells,) + square),
        disc_weight.reshape((cells,) + square),
        disc_head.reshape((cells,) + line),
    )
    return outs[0].reshape(gen_weight.shape), outs[1].reshape(disc_weight.shape), outs[2].reshape(disc_head.shape)


def solution(mesh):
    cells3, cells4 = P("gx", "gy", None), P("gx", "gy", None, None)
    return jax.shard_map(
        functools.partial(local, mesh.shape["gx"], mesh.shape["gy"]),
        mesh=mesh,
        in_specs=(P(), cells3, cells4, cells4, cells4, cells3),
        out_specs=(cells4, cells4, cells3),
        check_vma=False,
    )
```

```python
import functools

import jax
import jax.numpy as jnp
from jax import lax
from jax.experimental import pallas as pl
from jax.experimental.pallas import tpu as pltpu
from jax.sharding import PartitionSpec as P

F32 = jnp.float32
NN = ((1,), (0,))
NT = ((1,), (1,))
TN = ((0,), (0,))


def split(x):
    high = x.astype(jnp.bfloat16)
    return high, (x - high.astype(F32)).astype(jnp.bfloat16)


def dot3(a, b, dims):
    d = lambda x, y: lax.dot_general(x, y, (dims, ((), ())), preferred_element_type=F32)
    return d(a[0], b[0]) + (d(a[0], b[1]) + d(a[1], b[0]))


def descend(value, grad):
    mean_sq = jnp.sum(jnp.sum(grad * grad, 0, keepdims=True), 1, keepdims=True) * (1.0 / grad.size)
    return value - 0.25 * grad * lax.rsqrt(mean_sq + 1e-06)


def kernel(
    nx, ny, gxn, gyn,
    samples, idx, lat_in, gen_in, disc_in, head,
    gen_out, disc_out_ref, new_head,
    lat, gen, disc, new_gen, new_disc, table, real, disc_h, head_h, lat_h, made_in, made_out, fake, back, gw, gh, whi, wlo,
    table_sem, in_sems, out_sems, disc_s, disc_r, head_s, head_r, lat_s, lat_r, made_s, made_r,
):
    cells, rows, width = lat.shape
    slots = 2 * nx + 2 * ny
    scale = width ** (-0.5)
    gx, gy = lax.axis_index("gx"), lax.axis_index("gy")
    above, below = lax.rem(gx + gxn - 1, gxn), lax.rem(gx + 1, gxn)
    before, after = lax.rem(gy + gyn - 1, gyn), lax.rem(gy + 1, gyn)

    barrier = pltpu.get_barrier_semaphore()
    for there in ({"gx": above}, {"gx": below}, {"gy": before}, {"gy": after}):
        pl.semaphore_signal(barrier, inc=1, device_id=there, device_id_type=pl.DeviceIdType.MESH)
    loads = [
        pltpu.make_async_copy(src, dst, in_sems.at[k])
        for k, (src, dst) in enumerate(((disc_in, disc), (lat_in, lat), (gen_in, gen)))
    ]
    for load in loads:
        load.start()
    pl.semaphore_wait(barrier, 4)

    def remote(src, dst, send, recv, there):
        return pltpu.make_async_remote_copy(
            src_ref=src, dst_ref=dst, send_sem=send, recv_sem=recv,
            device_id=there, device_id_type=pl.DeviceIdType.MESH,
        )

    outgoing = []
    for i in range(nx):
        outgoing.append((2 * ny + i, i * ny + ny - 1, {"gy": after}))
        outgoing.append((2 * ny + nx + i, i * ny, {"gy": before}))
    for j in range(ny):
        outgoing.append((j, (nx - 1) * ny + j, {"gx": below}))
        outgoing.append((ny + j, j, {"gx": above}))

    head_out = [remote(head.at[c], head_h.at[s], head_s.at[s], head_r.at[s], t) for s, c, t in outgoing]
    disc_out = [remote(disc_in.at[c], disc_h.at[s], disc_s.at[s], disc_r.at[s], t) for s, c, t in outgoing]
    lat_out = [remote(lat_in.at[c], lat_h.at[s], lat_s.at[s], lat_r.at[s], t) for s, c, t in outgoing]
    for h, d in zip(head_out, disc_out):
        d.start()
        h.start()
    table_copy = pltpu.make_async_copy(samples, table, table_sem)
    table_copy.start()
    for load in loads:
        load.wait()

    def arrived(buf, sem, s):
        remote(buf.at[s], buf.at[s], sem.at[s], sem.at[s], {"gx": above}).wait_recv()

    def row_slot(t):
        d, i = lax.rem(t // nx + gy + 1, 2), lax.rem(t, nx)
        return d, 2 * ny + d * nx + i, 2 * ny + (1 - d) * nx + i, i * ny + d * (ny - 1)

    def col_slot(t):
        d, j = t // ny, lax.rem(t, ny)
        return d, d * ny + j, (1 - d) * ny + j, d * (nx - 1) * ny + j

    pair_loops = []
    if nx > 1:
        half = (nx - 1) * ny
        def vertical(t, half=half):
            b, d = lax.rem(t, half), t // half
            return b + d * ny, b + (1 - d) * ny
        pair_loops.append((2 * half, vertical))
    if ny > 1:
        wide = nx * (ny - 1)
        def horizontal(t, wide=wide):
            b, d = lax.rem(t, wide), t // wide
            at = (b // (ny - 1)) * ny + lax.rem(b, ny - 1)
            return at + d, at + 1 - d
        pair_loops.append((2 * wide, horizontal))

    def slope_inner(hidden, top, real_side):
        score = scale * jnp.sum(hidden * top, 1, keepdims=True)
        slope = -jax.nn.sigmoid(-score) if real_side else 0.2 * jax.nn.sigmoid(score)
        return slope, (1.0 - hidden * hidden) * ((scale * slope) * top)

    def opponent(x, w, top):
        hidden = jnp.tanh(scale * dot3(split(x), w, NN))
        _, inner = slope_inner(hidden, top, True)
        return scale * dot3(split(inner), w, NT)

    def critic(x, c, real_side):
        xs = split(x)
        top = head[c]
        hidden = jnp.tanh(scale * dot3(xs, (whi[c], wlo[c]), NN))
        slope, inner = slope_inner(hidden, top, real_side)
        return scale * dot3(xs, split(inner), TN), scale * jnp.sum(slope * hidden, 0, keepdims=True)

    def add_critic(x, c):
        term_w, term_h = critic(x, c, False)
        gw[c] += term_w
        gh[c] += term_h

    def make(source, g):
        return jnp.tanh(scale * dot3(split(source), split(new_gen[g]), NN))

    def own(c, _):
        whi[c], wlo[c] = split(disc[c])
        fake[c] = jnp.tanh(scale * dot3(split(lat[c]), split(gen[c]), NN))
        back[c] = opponent(fake[c], (whi[c], wlo[c]), head[c])
        return 0

    lax.fori_loop(0, cells, own, 0)
    for count, pair in pair_loops:
        def local_opponent(t, _, pair=pair):
            c, n = pair(t)
            back[c] += opponent(fake[c], (whi[n], wlo[n]), head[n])
            return 0
        lax.fori_loop(0, count, local_opponent, 0)

    table_copy.wait()

    def real_term(c, _):
        def fetch(b, _):
            for k in range(8):
                r = b * 8 + k
                real[pl.ds(r, 1), :] = table[pl.ds(idx[c // ny, lax.rem(c, ny), r], 1), :]
            return 0
        lax.fori_loop(0, rows // 8, fetch, 0)
        gw[c], gh[c] = critic(real[...], c, True)
        return 0

    lax.fori_loop(0, cells, real_term, 0)

    def far_opponent(where):
        def body(t, _):
            _, s, _, c = where(t)
            arrived(head_h, head_r, s)
            arrived(disc_h, disc_r, s)
            back[c] += opponent(fake[c], split(disc_h[s]), head_h[s])
            return 0
        return body

    lax.fori_loop(0, nx, far_opponent(row_slot), 0)
    for h, d, l in zip(head_out, disc_out, lat_out):
        h.wait_send()
        d.wait_send()
        l.start()
    lax.fori_loop(nx, 2 * nx, far_opponent(row_slot), 0)
    lax.fori_loop(0, 2 * ny, far_opponent(col_slot), 0)

    def store(src, dst, k, c):
        return pltpu.make_async_copy(src.at[c], dst.at[c], out_sems.at[k, c])

    def update(c, _):
        f = fake[c]
        grad = scale * dot3(split(lat[c]), split((1.0 - f * f) * back[c]), TN)
        new_gen[c] = descend(gen[c], grad)
        store(new_gen, gen_out, 0, c).start()
        return 0

    lax.fori_loop(0, cells, update, 0)

    def made_copy(where, axis, t):
        d, s, there, _ = where(t)
        me, n = (gx, gxn) if axis == "gx" else (gy, gyn)
        target = lax.rem(me + n + 2 * d - 1, n)
        return remote(made_out.at[s], made_in.at[there], made_s.at[s], made_r.at[there], {axis: target})

    def far_make(where, axis):
        def body(t, _):
            _, s, _, c = where(t)
            arrived(lat_h, lat_r, s)
            made_out[s] = make(lat_h[s], c)
            made_copy(where, axis, t).start()
            return 0
        return body

    lax.fori_loop(0, 2 * nx, far_make(row_slot, "gy"), 0)
    lax.fori_loop(0, 2 * ny, far_make(col_slot, "gx"), 0)

    def own_critic(c, _):
        add_critic(make(lat[c], c), c)
        return 0

    lax.fori_loop(0, cells, own_critic, 0)
    for count, pair in pair_loops:
        def local_critic(t, _, pair=pair):
            c, n = pair(t)
            add_critic(make(lat[c], n), c)
            return 0
        lax.fori_loop(0, count, local_critic, 0)

    def far_critic(where):
        def body(t, _):
            _, s, _, c = where(t)
            arrived(made_in, made_r, s)
            add_critic(made_in[s], c)
            return 0
        return body

    lax.fori_loop(0, 2 * nx, far_critic(row_slot), 0)
    lax.fori_loop(0, 2 * ny, far_critic(col_slot), 0)

    def finish(c, _):
        new_disc[c] = descend(disc[c], gw[c])
        store(new_disc, disc_out_ref, 1, c).start()
        new_head[c] = descend(head[c], gh[c])
        return 0

    lax.fori_loop(0, cells, finish, 0)
    for l in lat_out:
        l.wait_send()
    for t in range(2 * nx):
        made_copy(row_slot, "gy", t).wait_send()
    for t in range(2 * ny):
        made_copy(col_slot, "gx", t).wait_send()
    for c in range(cells):
        store(new_gen, gen_out, 0, c).wait()
        store(new_disc, disc_out_ref, 1, c).wait()


def local(gxn, gyn, samples, real_idx, latents, gen_weight, disc_weight, disc_head):
    nx, ny, rows, width = latents.shape
    cells, slots = nx * ny, 2 * (nx + ny)
    vmem, hbm = pl.BlockSpec(memory_space=pltpu.VMEM), pl.BlockSpec(memory_space=pl.ANY)
    square, block, line = (width, width), (rows, width), (1, width)
    dma = lambda: pltpu.SemaphoreType.DMA((slots,))
    outs = pl.pallas_call(
        functools.partial(kernel, nx, ny, gxn, gyn),
        out_shape=(
            jax.ShapeDtypeStruct((cells,) + square, F32),
            jax.ShapeDtypeStruct((cells,) + square, F32),
            jax.ShapeDtypeStruct((cells,) + line, F32),
        ),
        in_specs=[hbm, pl.BlockSpec(memory_space=pltpu.SMEM), hbm, hbm, hbm, vmem],
        out_specs=(hbm, hbm, vmem),
        scratch_shapes=[
            pltpu.VMEM((cells,) + block, F32),
            pltpu.VMEM((cells,) + square, F32),
            pltpu.VMEM((cells,) + square, F32),
            pltpu.VMEM((cells,) + square, F32),
            pltpu.VMEM((cells,) + square, F32),
            pltpu.VMEM(samples.shape, F32),
            pltpu.VMEM(block, F32),
            pltpu.VMEM((slots,) + square, F32),
            pltpu.VMEM((slots,) + line, F32),
            pltpu.VMEM((slots,) + block, F32),
            pltpu.VMEM((slots,) + block, F32),
            pltpu.VMEM((slots,) + block, F32),
            pltpu.VMEM((cells,) + block, F32),
            pltpu.VMEM((cells,) + block, F32),
            pltpu.VMEM((cells,) + square, F32),
            pltpu.VMEM((cells,) + line, F32),
            pltpu.VMEM((cells,) + square, jnp.bfloat16),
            pltpu.VMEM((cells,) + square, jnp.bfloat16),
            pltpu.SemaphoreType.DMA,
            pltpu.SemaphoreType.DMA((3,)),
            pltpu.SemaphoreType.DMA((2, cells)),
        ] + [dma() for _ in range(8)],
        compiler_params=pltpu.CompilerParams(
            collective_id=0, has_side_effects=True, vmem_limit_bytes=58 * 1024 * 1024
        ),
        name="coev",
    )(
        samples,
        real_idx,
        latents.reshape((cells,) + block),
        gen_weight.reshape((cells,) + square),
        disc_weight.reshape((cells,) + square),
        disc_head.reshape((cells,) + line),
    )
    return outs[0].reshape(gen_weight.shape), outs[1].reshape(disc_weight.shape), outs[2].reshape(disc_head.shape)


def solution(mesh):
    cells3, cells4 = P("gx", "gy", None), P("gx", "gy", None, None)
    return jax.shard_map(
        functools.partial(local, mesh.shape["gx"], mesh.shape["gy"]),
        mesh=mesh,
        in_specs=(P(), cells3, cells4, cells4, cells4, cells3),
        out_specs=(cells4, cells4, cells3),
        check_vma=False,
    )
```

```python
import functools

import jax
import jax.numpy as jnp
from jax import lax
from jax.experimental import pallas as pl
from jax.experimental.pallas import tpu as pltpu
from jax.sharding import PartitionSpec as P

F32 = jnp.float32
NN = ((1,), (0,))
NT = ((1,), (1,))
TN = ((0,), (0,))


def split(x):
    high = x.astype(jnp.bfloat16)
    return high, (x - high.astype(F32)).astype(jnp.bfloat16)


def dot3(a, b, dims):
    d = lambda x, y: lax.dot_general(x, y, (dims, ((), ())), preferred_element_type=F32)
    return d(a[0], b[0]) + (d(a[0], b[1]) + d(a[1], b[0]))


def descend(value, grad):
    mean_sq = jnp.sum(jnp.sum(grad * grad, 0, keepdims=True), 1, keepdims=True) * (1.0 / grad.size)
    return value - 0.25 * grad * lax.rsqrt(mean_sq + 1e-06)


def kernel(
    nx, ny, gxn, gyn,
    samples, idx, lat_in, gen_in, disc_in, head,
    gen_out, disc_out_ref, new_head,
    lat, gen, disc, new_gen, new_disc, table, real, disc_h, head_h, lat_h, made_in, made_out, fake, back, gw, gh, whi, wlo,
    table_sem, in_sems, out_sems, disc_s, disc_r, head_s, head_r, lat_s, lat_r, made_s, made_r,
):
    cells, rows, width = lat.shape
    slots = 2 * nx + 2 * ny
    scale = width ** (-0.5)
    gx, gy = lax.axis_index("gx"), lax.axis_index("gy")
    above, below = lax.rem(gx + gxn - 1, gxn), lax.rem(gx + 1, gxn)
    before, after = lax.rem(gy + gyn - 1, gyn), lax.rem(gy + 1, gyn)

    barrier = pltpu.get_barrier_semaphore()
    for there in ({"gx": above}, {"gx": below}, {"gy": before}, {"gy": after}):
        pl.semaphore_signal(barrier, inc=1, device_id=there, device_id_type=pl.DeviceIdType.MESH)
    loads = [
        pltpu.make_async_copy(src, dst, in_sems.at[k])
        for k, (src, dst) in enumerate(((disc_in, disc), (lat_in, lat), (gen_in, gen)))
    ]
    for load in loads:
        load.start()
    pl.semaphore_wait(barrier, 4)

    def remote(src, dst, send, recv, there):
        return pltpu.make_async_remote_copy(
            src_ref=src, dst_ref=dst, send_sem=send, recv_sem=recv,
            device_id=there, device_id_type=pl.DeviceIdType.MESH,
        )

    outgoing = []
    for i in range(nx):
        outgoing.append((2 * ny + i, i * ny + ny - 1, {"gy": after}))
        outgoing.append((2 * ny + nx + i, i * ny, {"gy": before}))
    for j in range(ny):
        outgoing.append((j, (nx - 1) * ny + j, {"gx": below}))
        outgoing.append((ny + j, j, {"gx": above}))

    head_out = [remote(head.at[c], head_h.at[s], head_s.at[s], head_r.at[s], t) for s, c, t in outgoing]
    disc_out = [remote(disc_in.at[c], disc_h.at[s], disc_s.at[s], disc_r.at[s], t) for s, c, t in outgoing]
    lat_out = [remote(lat_in.at[c], lat_h.at[s], lat_s.at[s], lat_r.at[s], t) for s, c, t in outgoing]
    for h, d in zip(head_out, disc_out):
        d.start()
        h.start()
    table_copy = pltpu.make_async_copy(samples, table, table_sem)
    table_copy.start()
    for load in loads:
        load.wait()

    def arrived(buf, sem, s):
        remote(buf.at[s], buf.at[s], sem.at[s], sem.at[s], {"gx": above}).wait_recv()

    def row_slot(t):
        d, i = lax.rem(t // nx + gy + 1, 2), lax.rem(t, nx)
        return d, 2 * ny + d * nx + i, 2 * ny + (1 - d) * nx + i, i * ny + d * (ny - 1)

    def col_slot(t):
        d, j = t // ny, lax.rem(t, ny)
        return d, d * ny + j, (1 - d) * ny + j, d * (nx - 1) * ny + j

    pair_loops = []
    if nx > 1:
        half = (nx - 1) * ny
        def vertical(t, half=half):
            b, d = lax.rem(t, half), t // half
            return b + d * ny, b + (1 - d) * ny
        pair_loops.append((2 * half, vertical))
    if ny > 1:
        wide = nx * (ny - 1)
        def horizontal(t, wide=wide):
            b, d = lax.rem(t, wide), t // wide
            at = (b // (ny - 1)) * ny + lax.rem(b, ny - 1)
            return at + d, at + 1 - d
        pair_loops.append((2 * wide, horizontal))

    def slope_inner(hidden, top, real_side):
        score = scale * jnp.sum(hidden * top, 1, keepdims=True)
        slope = -jax.nn.sigmoid(-score) if real_side else 0.2 * jax.nn.sigmoid(score)
        return slope, (1.0 - hidden * hidden) * ((scale * slope) * top)

    def opponent(x, w, top):
        hidden = jnp.tanh(scale * dot3(split(x), w, NN))
        _, inner = slope_inner(hidden, top, True)
        return scale * dot3(split(inner), w, NT)

    def critic(x, c, real_side):
        xs = split(x)
        top = head[c]
        hidden = jnp.tanh(scale * dot3(xs, (whi[c], wlo[c]), NN))
        slope, inner = slope_inner(hidden, top, real_side)
        return scale * dot3(xs, split(inner), TN), scale * jnp.sum(slope * hidden, 0, keepdims=True)

    def add_critic(x, c):
        term_w, term_h = critic(x, c, False)
        gw[c] += term_w
        gh[c] += term_h

    def make(source, g):
        return jnp.tanh(scale * dot3(split(source), split(new_gen[g]), NN))

    def own(c, _):
        whi[c], wlo[c] = split(disc[c])
        fake[c] = jnp.tanh(scale * dot3(split(lat[c]), split(gen[c]), NN))
        back[c] = opponent(fake[c], (whi[c], wlo[c]), head[c])
        return 0

    lax.fori_loop(0, cells, own, 0)
    for count, pair in pair_loops:
        def local_opponent(t, _, pair=pair):
            c, n = pair(t)
            back[c] += opponent(fake[c], (whi[n], wlo[n]), head[n])
            return 0
        lax.fori_loop(0, count, local_opponent, 0)

    table_copy.wait()

    def real_term(c, _):
        def fetch(b, _):
            for k in range(8):
                r = b * 8 + k
                real[pl.ds(r, 1), :] = table[pl.ds(idx[c // ny, lax.rem(c, ny), r], 1), :]
            return 0
        lax.fori_loop(0, rows // 8, fetch, 0)
        gw[c], gh[c] = critic(real[...], c, True)
        return 0

    lax.fori_loop(0, cells, real_term, 0)

    def far_opponent(where):
        def body(t, _):
            _, s, _, c = where(t)
            arrived(head_h, head_r, s)
            arrived(disc_h, disc_r, s)
            back[c] += opponent(fake[c], split(disc_h[s]), head_h[s])
            return 0
        return body

    lax.fori_loop(0, nx, far_opponent(row_slot), 0)
    for h, d, l in zip(head_out, disc_out, lat_out):
        h.wait_send()
        d.wait_send()
        l.start()
    lax.fori_loop(nx, 2 * nx, far_opponent(row_slot), 0)
    lax.fori_loop(0, 2 * ny, far_opponent(col_slot), 0)

    def store(src, dst, k, c):
        return pltpu.make_async_copy(src.at[c], dst.at[c], out_sems.at[k, c])

    def update(c, _):
        f = fake[c]
        grad = scale * dot3(split(lat[c]), split((1.0 - f * f) * back[c]), TN)
        new_gen[c] = descend(gen[c], grad)
        store(new_gen, gen_out, 0, c).start()
        return 0

    lax.fori_loop(0, cells, update, 0)

    def made_copy(where, axis, t):
        d, s, there, _ = where(t)
        me, n = (gx, gxn) if axis == "gx" else (gy, gyn)
        target = lax.rem(me + n + 2 * d - 1, n)
        return remote(made_out.at[s], made_in.at[there], made_s.at[s], made_r.at[there], {axis: target})

    def far_make(where, axis, send):
        def body(t, _):
            _, s, _, c = where(t)
            arrived(lat_h, lat_r, s)
            made_out[s] = make(lat_h[s], c)
            if send:
                made_copy(where, axis, t).start()
            return 0
        return body

    mid = nx + (nx + 1) // 2
    lax.fori_loop(0, mid, far_make(row_slot, "gy", True), 0)
    lax.fori_loop(0, ny, far_make(col_slot, "gx", True), 0)
    lax.fori_loop(mid, 2 * nx, far_make(row_slot, "gy", False), 0)
    lax.fori_loop(ny, 2 * ny, far_make(col_slot, "gx", False), 0)

    def own_critic(c, _):
        add_critic(make(lat[c], c), c)
        return 0

    lax.fori_loop(0, cells, own_critic, 0)
    for count, pair in pair_loops:
        def local_critic(t, _, pair=pair):
            c, n = pair(t)
            add_critic(make(lat[c], n), c)
            return 0
        lax.fori_loop(0, count, local_critic, 0)

    for t in range(mid):
        made_copy(row_slot, "gy", t).wait_send()
    for t in range(mid, 2 * nx):
        made_copy(row_slot, "gy", t).start()
    for t in range(ny):
        made_copy(col_slot, "gx", t).wait_send()
    for t in range(ny, 2 * ny):
        made_copy(col_slot, "gx", t).start()

    def far_critic(where):
        def body(t, _):
            _, s, _, c = where(t)
            arrived(made_in, made_r, s)
            add_critic(made_in[s], c)
            return 0
        return body

    def far_row(t, _):
        return far_critic(row_slot)(t, 0)

    lax.fori_loop(0, mid, far_row, 0)
    lax.fori_loop(0, ny, lambda t, _: far_critic(col_slot)(lax.rem(t + ny, 2 * ny), 0), 0)
    lax.fori_loop(mid, 2 * nx, far_row, 0)
    lax.fori_loop(ny, 2 * ny, lambda t, _: far_critic(col_slot)(t - ny, 0), 0)

    def finish(c, _):
        new_disc[c] = descend(disc[c], gw[c])
        store(new_disc, disc_out_ref, 1, c).start()
        new_head[c] = descend(head[c], gh[c])
        return 0

    lax.fori_loop(0, cells, finish, 0)
    for l in lat_out:
        l.wait_send()
    for t in range(mid, 2 * nx):
        made_copy(row_slot, "gy", t).wait_send()
    for t in range(ny, 2 * ny):
        made_copy(col_slot, "gx", t).wait_send()
    for c in range(cells):
        store(new_gen, gen_out, 0, c).wait()
        store(new_disc, disc_out_ref, 1, c).wait()


def hand_over(gen_in, disc_in, head_in, gen_out, disc_out, head_out, sems):
    copies = [pltpu.make_async_copy(head_in, head_out, sems.at[2, 0, 0])]
    cells, width, _ = gen_in.shape
    half = width // 2
    for k, (src, dst) in enumerate(((gen_in, gen_out), (disc_in, disc_out))):
        for c in range(cells):
            for p in range(2):
                part = pl.ds(p * half, half)
                copies.append(pltpu.make_async_copy(src.at[c, part], dst.at[c, part], sems.at[k, c, p]))
    for copy in copies:
        copy.start()
    for copy in copies:
        copy.wait()


def local(gxn, gyn, samples, real_idx, latents, gen_weight, disc_weight, disc_head):
    nx, ny, rows, width = latents.shape
    cells, slots = nx * ny, 2 * (nx + ny)
    vmem, hbm = pl.BlockSpec(memory_space=pltpu.VMEM), pl.BlockSpec(memory_space=pl.ANY)
    square, block, line = (width, width), (rows, width), (1, width)
    dma = lambda: pltpu.SemaphoreType.DMA((slots,))
    outs = pl.pallas_call(
        functools.partial(kernel, nx, ny, gxn, gyn),
        out_shape=(
            jax.ShapeDtypeStruct((cells,) + square, F32),
            jax.ShapeDtypeStruct((cells,) + square, F32),
            jax.ShapeDtypeStruct((cells,) + line, F32),
        ),
        in_specs=[hbm, pl.BlockSpec(memory_space=pltpu.SMEM), hbm, hbm, hbm, vmem],
        out_specs=(hbm, hbm, vmem),
        scratch_shapes=[
            pltpu.VMEM((cells,) + block, F32),
            pltpu.VMEM((cells,) + square, F32),
            pltpu.VMEM((cells,) + square, F32),
            pltpu.VMEM((cells,) + square, F32),
            pltpu.VMEM((cells,) + square, F32),
            pltpu.VMEM(samples.shape, F32),
            pltpu.VMEM(block, F32),
            pltpu.VMEM((slots,) + square, F32),
            pltpu.VMEM((slots,) + line, F32),
            pltpu.VMEM((slots,) + block, F32),
            pltpu.VMEM((slots,) + block, F32),
            pltpu.VMEM((slots,) + block, F32),
            pltpu.VMEM((cells,) + block, F32),
            pltpu.VMEM((cells,) + block, F32),
            pltpu.VMEM((cells,) + square, F32),
            pltpu.VMEM((cells,) + line, F32),
            pltpu.VMEM((cells,) + square, jnp.bfloat16),
            pltpu.VMEM((cells,) + square, jnp.bfloat16),
            pltpu.SemaphoreType.DMA,
            pltpu.SemaphoreType.DMA((3,)),
            pltpu.SemaphoreType.DMA((2, cells)),
        ] + [dma() for _ in range(8)],
        compiler_params=pltpu.CompilerParams(
            collective_id=0, has_side_effects=True, vmem_limit_bytes=58 * 1024 * 1024
        ),
        name="coev",
    )(
        samples,
        real_idx,
        latents.reshape((cells,) + block),
        gen_weight.reshape((cells,) + square),
        disc_weight.reshape((cells,) + square),
        disc_head.reshape((cells,) + line),
    )
    outs = pl.pallas_call(
        hand_over,
        out_shape=tuple(jax.ShapeDtypeStruct(o.shape, F32) for o in outs),
        in_specs=[hbm] * 3,
        out_specs=(hbm,) * 3,
        scratch_shapes=[pltpu.SemaphoreType.DMA((3, cells, 2))],
        name="hand_over",
    )(*outs)
    return outs[0].reshape(gen_weight.shape), outs[1].reshape(disc_weight.shape), outs[2].reshape(disc_head.shape)


def solution(mesh):
    cells3, cells4 = P("gx", "gy", None), P("gx", "gy", None, None)
    return jax.shard_map(
        functools.partial(local, mesh.shape["gx"], mesh.shape["gy"]),
        mesh=mesh,
        in_specs=(P(), cells3, cells4, cells4, cells4, cells3),
        out_specs=(cells4, cells4, cells3),
        check_vma=False,
    )
```
